256 devices in a mesh: dp: 32 (over x, z), tensor: 8 (over y, core).
Axes of the slice: x: 4, y: 4, z: 8, core: 2. Of those that a mesh axis runs over, the one named last changes fastest.
Arguments:
- activations: bfloat16 [65536, 4096], P('dp', 'tensor'), may hold values from -6 to 6
- hidden_grads: bfloat16 [65536, 14336], P('dp', 'tensor'), may hold values from -6 to 6
- basis_in: bfloat16 [4096, 64], P('tensor'), may hold values from -0.09375 to 0.09375
- basis_out: bfloat16 [14336, 64], P('tensor'), may hold values from -0.046875 to 0.046875
- precond_out: float32 [64, 64], replicated, may hold values from -0.75 to 0.75
- precond_in: float32 [64, 64], replicated, may hold values from -0.75 to 0.75
- lengths: int32 [128], P('dp'), may hold values from 128 to 512, as said below
- query_ids: int32 [1024], replicated, may hold values from 0 to 127
Outputs:
- scores: float32 [128, 1024], P('dp', 'tensor')
The draws below stay inside these ranges and needn't reach their ends.
Inputs may be any that keep to these rules, and one draw needn't show every extreme that they name: `lengths`: each block of 4 consecutive examples holds one of length 512.
All inputs are finite; a program needn't handle non-finite values.
Results may differ from the reference program's by a relative error of at most 0.0003.
Values sent between devices are 32-bit elements; how exact they have to be, the bound alone decides.
A program may use at most 64 MiB of HBM per device.

```python
import jax
import jax.numpy as jnp
from jax import lax

D = 4096
FF = 14336
R = 64
SEQ_LEN = 512
SEQ_DEV = 4
Q = 1024
B = 128
TOKENS = 65536


def draw_lengths(key, part):
    key = jax.random.fold_in(key, 1)
    first_key, second_key = jax.random.split(key)
    counts = jax.random.randint(first_key, (B,), SEQ_LEN // 4, SEQ_LEN + 1)
    picked = jax.random.randint(second_key, (B // SEQ_DEV,), 0, SEQ_DEV)
    within = jnp.arange(B) % SEQ_DEV
    full_slot = within == jnp.repeat(picked, SEQ_DEV, total_repeat_length=B)
    return jnp.where(full_slot, SEQ_LEN, counts).astype(jnp.int32)


def with_ends(values, rng, low, top_value):
    longest = values.shape.index(max(values.shape))
    spots = []
    for shift in (0, 1):
        where = [jax.random.randint(jax.random.fold_in(rng, axis), (), 0, length) for axis, length in enumerate(values.shape)]
        where[longest] = (where[longest] + shift) % values.shape[longest]
        spots.append(tuple(where))
    return values.at[spots[0]].set(low).at[spots[1]].set(top_value)


def steps_of(rng, dims, pieces, smallest, high):
    def one(position, shards_of):
        draws = jax.random.uniform(jax.random.fold_in(jax.random.fold_in(rng, 6), position), (shards_of,), jnp.float32, smallest / len(pieces), high / len(pieces))
        return jnp.repeat(jnp.exp(draws), dims[position] // shards_of).reshape((-1,) + (1,) * (len(dims) - position - 1))

    loudness = one(*pieces[0])
    for cut in pieces[1:]:
        loudness = loudness * one(*cut)
    return loudness


def noise(rng, dims, width, bound, pieces=(), held_as=jnp.bfloat16):
    drawn = width * jax.random.normal(rng, dims, jnp.float32)
    if pieces:
        drawn = drawn * steps_of(rng, dims, pieces, -0.22, 0.18)
    return jnp.clip(drawn, -bound, bound).astype(held_as)


def setup_inputs(seed: int = 0) -> dict:
    arg_keys = jax.random.split(jax.random.key(seed), 9)
    activations = noise(arg_keys[0], (TOKENS, D), 1.0, 6.0, ((0, 32), (1, 8)))
    hidden_grads = noise(arg_keys[1], (TOKENS, FF), 1.0, 6.0, ((0, 32), (1, 8)))
    basis_in = noise(arg_keys[2], (D, R), D ** -0.5, 0.09375, ((0, 8),))
    basis_out = noise(arg_keys[3], (FF, R), FF ** -0.5, 0.046875, ((0, 8),))
    precond_out = noise(arg_keys[4], (R, R), R ** -0.5, 0.75, (), jnp.float32)
    precond_in = noise(arg_keys[5], (R, R), R ** -0.5, 0.75, (), jnp.float32)
    lengths = draw_lengths(jax.random.fold_in(arg_keys[8], 71), 0)
    query_ids = with_ends(jax.random.randint(arg_keys[7], (Q,), 0, B), jax.random.fold_in(arg_keys[7], 1), 0, B - 1).astype(jnp.int32)
    return {"activations": activations, "hidden_grads": hidden_grads, "basis_in": basis_in, "basis_out": basis_out, "precond_out": precond_out, "precond_in": precond_in, "lengths": lengths, "query_ids": query_ids}


def reference(activations, hidden_grads, basis_in, basis_out, precond_out, precond_in, lengths, query_ids):
    acts = activations.reshape(B, SEQ_LEN, D)
    grads = hidden_grads.reshape(B, SEQ_LEN, FF)
    scale = 1.0 / (SEQ_LEN ** 0.5)
    wide_in = basis_in.astype(jnp.float32)
    wide_out = basis_out.astype(jnp.float32)

    def one_example(items):
        act_rows, grad_rows, length = items
        live = (jnp.arange(SEQ_LEN, dtype=jnp.int32) < length).astype(jnp.float32)
        proj_act = jnp.dot(act_rows.astype(jnp.float32), wide_in, precision=lax.Precision.HIGHEST) * live[:, None]
        proj_grad = jnp.dot(grad_rows.astype(jnp.float32), wide_out, precision=lax.Precision.HIGHEST)
        return jnp.dot(proj_grad.T, proj_act, precision=lax.Precision.HIGHEST) * scale

    sketch = lax.map(one_example, (acts, grads, lengths))
    left = jnp.einsum("ij,bjk->bik", precond_out, sketch, precision=lax.Precision.HIGHEST)
    precond = jnp.einsum("bik,kl->bil", left, precond_in, precision=lax.Precision.HIGHEST)
    chosen = sketch[query_ids]
    return jnp.einsum("bij,qij->bq", precond, chosen, precision=lax.Precision.HIGHEST) / R
```

```python
import jax
import jax.numpy as jnp
from jax import lax
from jax.experimental import pallas as pl
from jax.experimental.pallas import tpu as pltpu
from jax.sharding import PartitionSpec as P

MESH = pl.DeviceIdType.MESH
NX, NY, NZ = 4, 4, 8
RANK = 64
OFFSETS = (2, 1, 3, 0)
Z_ARRIVAL = (1, 7, 2, 6, 3, 5, 4)
Z_SEND = (4, 3, 5, 2, 6, 1, 7)
WINDOW = 3
F32 = jnp.float32
BF16 = jnp.bfloat16
NN = (((1,), (0,)), ((), ()))
NT = (((1,), (1,)), ((), ()))
TN = (((0,), (0,)), ((), ()))


def split(value):
    high = value.astype(BF16)
    return high, (value - high.astype(F32)).astype(BF16)


def dot(left, right, dims):
    return lax.dot_general(left, right, dims, preferred_element_type=F32)


def dot_split(left, right, dims):
    left_high, left_low = left
    right_high, right_low = right
    return dot(left_high, right_high, dims) + (
        dot(left_high, right_low, dims) + dot(left_low, right_high, dims)
    )


def kernel(
    act_hbm, grad_hbm, basis_in_hbm, basis_out_hbm, left_hbm, right_hbm, lengths_hbm, ids_hbm,
    out_ref,
    act, grad, basis, left, right, lengths, ids,
    part, pair, gathered, sketch_part, sketch_pair, sketches, preconds, precond_own, score_own, scores,
    load_sem, small_sem, core_send, core_recv, y_send, y_recv, z_send, z_recv, x_send, x_recv,
    p_send, p_recv, f_send, f_recv,
):
    dp = lax.axis_index("dp")
    tensor = lax.axis_index("tensor")
    x, z = dp // NZ, dp % NZ
    y, core = tensor // 2, tensor % 2
    other = 1 - core

    def device(dx, dy, dz, flip):
        to_core = other if flip else core
        return (
            lax.rem(x + dx, NX) * NZ + lax.rem(z + dz, NZ),
            lax.rem(y + dy, NY) * 2 + to_core,
        )

    def remote(src, dst, send, recv, target):
        return pltpu.make_async_remote_copy(
            src_ref=src, dst_ref=dst, send_sem=send, recv_sem=recv,
            device_id=target, device_id_type=MESH,
        )

    half = part.shape[2]
    small = [
        pltpu.make_async_copy(
            basis_in_hbm, basis.at[pl.ds(0, RANK), pl.ds(0, act.shape[1])], small_sem.at[0]
        ),
        pltpu.make_async_copy(
            basis_out_hbm,
            basis.at[pl.ds(RANK, RANK), pl.ds(act.shape[1], grad.shape[1])],
            small_sem.at[1],
        ),
        pltpu.make_async_copy(left_hbm, left, small_sem.at[2]),
        pltpu.make_async_copy(right_hbm, right, small_sem.at[3]),
        pltpu.make_async_copy(lengths_hbm, lengths, small_sem.at[4]),
        pltpu.make_async_copy(ids_hbm, ids, small_sem.at[5]),
    ]

    def rows_of(index):
        step, mine = index // 2, index % 2
        example = lax.rem(y + OFFSETS[step], NY)
        return pl.ds(pl.multiple_of((example * 2 + (core if mine else other)) * half, half), half)

    def loads(index):
        rows = rows_of(index)
        return (
            pltpu.make_async_copy(act_hbm.at[rows], act.at[rows], load_sem.at[0, index]),
            pltpu.make_async_copy(grad_hbm.at[rows], grad.at[rows], load_sem.at[1, index]),
        )

    small[0].start()
    small[1].start()
    for index in range(WINDOW):
        for copy in loads(index):
            copy.start()
    for copy in small[2:]:
        copy.start()

    barrier = pltpu.get_barrier_semaphore()
    partners = [(0, dy, 0, flip) for dy in range(NY) for flip in (0, 1) if dy or flip]
    partners += [(0, 0, dz, 0) for dz in range(1, NZ)]
    partners += [(dx, 0, 0, 0) for dx in range(1, NX)]
    for partner in partners:
        pl.semaphore_signal(barrier, 1, device_id=device(*partner), device_id_type=MESH)

    basis[0:RANK, act.shape[1] :] = jnp.zeros((RANK, grad.shape[1]), BF16)
    basis[RANK:, 0 : act.shape[1]] = jnp.zeros((RANK, act.shape[1]), BF16)
    small[0].wait()
    small[1].wait()

    def project(index):
        for copy in loads(index):
            copy.wait()
        if index + WINDOW < 2 * len(OFFSETS):
            for copy in loads(index + WINDOW):
                copy.start()
        rows = rows_of(index)
        part[index // 2, index % 2] = dot(act[rows, :], basis[:, 0 : act.shape[1]], NT) + dot(
            grad[rows, :], basis[:, act.shape[1] :], NT
        )

    def to_core(step):
        return remote(
            part.at[step, 0], pair.at[step], core_send.at[step], core_recv.at[step],
            device(0, 0, 0, 1),
        )

    def to_chip(step):
        return remote(
            part.at[step, 1], gathered.at[step], y_send.at[step], y_recv.at[step],
            device(0, OFFSETS[step], 0, 0),
        )

    def merge(step):
        to_core(step).wait_recv()
        part[step, 1] = part[step, 1] + pair[step]
        if OFFSETS[step]:
            to_chip(step).start()

    for step in range(len(OFFSETS)):
        project(2 * step)
        if step == 0:
            pl.semaphore_wait(barrier, len(partners))
        to_core(step).start()
        project(2 * step + 1)
        if step:
            merge(step - 1)
    merge(len(OFFSETS) - 1)

    last = len(OFFSETS) - 1
    for copy in small[2:]:
        copy.wait()
    left_split = split(left[...])
    right_split = split(right[...])
    total = part[last, 1]
    for step in range(last):
        to_chip(step).wait_recv()
        total = total + gathered[step]
    slot = lax.broadcasted_iota(jnp.int32, total.shape, 0) + core * half
    total = jnp.where(slot < lengths[y], total, 0.0)
    total_split = split(total)
    square = dot_split(total_split, total_split, TN)
    corner = square[RANK:, 0:RANK]
    sketch_part[...] = jnp.concatenate([corner[: RANK // 2], corner[RANK // 2 :]], axis=1)
    swap = remote(
        sketch_part, sketch_pair, core_send.at[last + 1], core_recv.at[last + 1],
        device(0, 0, 0, 1),
    )
    swap.start()
    swap.wait_recv()
    packed = sketch_part[...] + sketch_pair[...]
    sketch_pair[...] = packed

    block = RANK // 4

    def place(at_x, at_z):
        return sketches.at[pl.ds(pl.multiple_of((at_x * NZ + at_z) * block, block), block)]

    own_rows = pl.ds(pl.multiple_of(core * block, block), block)
    sketches[pl.ds(pl.multiple_of((x * NZ + z) * block, block), block), :] = sketch_pair[own_rows, :]
    own = place(x, z)

    def to_z(dz):
        return remote(own, own, z_send.at[dz], z_recv.at[dz], device(0, 0, dz, 0))

    def from_z(dz):
        spot = place(x, lax.rem(z + NZ - dz, NZ))
        return remote(spot, spot, z_send.at[dz], z_recv.at[dz], device(0, 0, dz, 0))

    def to_x(dx, dz):
        spot = place(x, lax.rem(z + NZ - dz, NZ))
        return remote(spot, spot, x_send.at[dx, dz], x_recv.at[dx, dz], device(dx, 0, 0, 0))

    def from_x(dx, dz):
        spot = place(lax.rem(x + NX - dx, NX), lax.rem(z + NZ - dz, NZ))
        return remote(spot, spot, x_send.at[dx, dz], x_recv.at[dx, dz], device(dx, 0, 0, 0))

    for dz in Z_SEND:
        to_z(dz).start()
    for dx in (2, 1, 3):
        to_x(dx, 0).start()

    whole = jnp.concatenate([packed[:, 0:RANK], packed[:, RANK:]], axis=0)
    halfway = dot_split(split(whole), right_split, NN)
    precond = dot_split(left_split, split(halfway), NN)
    precond_own[...] = jnp.concatenate([precond[: RANK // 2], precond[RANK // 2 :]], axis=1)

    def p_place(at_y):
        return preconds.at[pl.ds(pl.multiple_of(at_y * block, block), block)]

    preconds[pl.ds(pl.multiple_of(y * block, block), block), :] = precond_own[own_rows, :]

    def to_y(dy):
        return remote(p_place(y), p_place(y), p_send.at[dy], p_recv.at[dy], device(0, dy, 0, 0))

    def from_y(dy):
        spot = p_place(lax.rem(y + NY - dy, NY))
        return remote(spot, spot, p_send.at[dy], p_recv.at[dy], device(0, dy, 0, 0))

    for dy in (2, 1, 3):
        to_y(dy).start()

    for dz in Z_ARRIVAL:
        from_z(dz).wait_recv()
        for dx in (2, 1, 3):
            to_x(dx, dz).start()
    for dy in range(1, NY):
        from_y(dy).wait_recv()
    weights = split(
        jnp.concatenate([preconds[pl.ds(row, NY, stride=block), :] for row in range(block)], axis=1)
    )
    for dz in (0,) + Z_ARRIVAL:
        for dx in (1, 3, 2):
            from_x(dx, dz).wait_recv()
    rows = NX * NZ
    found = split(
        jnp.concatenate([sketches[pl.ds(row, rows, stride=block), :] for row in range(block)], axis=1)
    )
    found = [jnp.concatenate([term] * NY, axis=0) for term in found]
    lane = lax.broadcasted_iota(jnp.int32, (NY, rows * NY), 1)
    mine = jnp.where(lane // rows == y, dot_split(weights, found, NT), 0.0)

    score_own[0:NY, :] = mine
    score_own[NY:, :] = jnp.zeros((8 - NY, rows * NY), F32)

    def exchange(dy, flip):
        index = dy * 2 + flip
        return remote(
            score_own, scores.at[index], f_send.at[index], f_recv.at[index], device(0, dy, 0, flip)
        )

    everyone = [(dy, flip) for dy in (2, 1, 3, 0) for flip in (1, 0) if dy or flip]
    for pair_to in everyone:
        exchange(*pair_to).start()
    query = ids[pl.ds(tensor, 1), :]
    spot = lax.broadcasted_iota(jnp.int32, (rows * NY, rows * NY), 0)
    onehot = jnp.where(spot % rows * NY + spot // rows == query, 1.0, 0.0).astype(BF16)
    table = score_own[...]
    for pair_to in everyone[::-1]:
        exchange(*pair_to).wait_recv()
    for pair_to in everyone:
        table = table + scores[pair_to[0] * 2 + pair_to[1]]
    high, low = split(table)
    lowest = (table - high.astype(F32) - low.astype(F32)).astype(BF16)
    picked = dot(high, onehot, NN) + (dot(low, onehot, NN) + dot(lowest, onehot, NN))
    out_ref[...] = picked[0:NY, :] * (1.0 / (2 * half * RANK))

    for step in range(len(OFFSETS)):
        to_core(step).wait_send()
        if OFFSETS[step]:
            to_chip(step).wait_send()
    swap.wait_send()
    for dz in Z_SEND:
        to_z(dz).wait_send()
    for dz in range(NZ):
        for dx in range(1, NX):
            to_x(dx, dz).wait_send()
    for dy in range(1, NY):
        to_y(dy).wait_send()
    for pair_to in everyone:
        exchange(*pair_to).wait_send()


def local(
    activations, hidden_grads, basis_in, basis_out, precond_out, precond_in, lengths, query_ids
):
    tokens, features = activations.shape
    hidden = hidden_grads.shape[1]
    half = tokens // (2 * NY)
    dma = pltpu.SemaphoreType.DMA
    return pl.pallas_call(
        kernel,
        out_shape=jax.ShapeDtypeStruct((NY, query_ids.shape[0] // (2 * NY)), F32),
        in_specs=[pl.BlockSpec(memory_space=pltpu.HBM)] * 8,
        out_specs=pl.BlockSpec(memory_space=pltpu.VMEM),
        scratch_shapes=[
            pltpu.VMEM((tokens, features), BF16),
            pltpu.VMEM((tokens, hidden), BF16),
            pltpu.VMEM((2 * RANK, features + hidden), BF16),
            pltpu.VMEM((RANK, RANK), F32),
            pltpu.VMEM((RANK, RANK), F32),
            pltpu.SMEM((NY,), jnp.int32),
            pltpu.VMEM((2 * NY, query_ids.shape[0] // (2 * NY)), jnp.int32),
            pltpu.VMEM((NY, 2, half, 2 * RANK), F32),
            pltpu.VMEM((NY, half, 2 * RANK), F32),
            pltpu.VMEM((NY - 1, half, 2 * RANK), F32),
            pltpu.VMEM((RANK // 2, 2 * RANK), F32),
            pltpu.VMEM((RANK // 2, 2 * RANK), F32),
            pltpu.VMEM((NX * NZ * RANK // 4, 2 * RANK), F32),
            pltpu.VMEM((NY * RANK // 4, 2 * RANK), F32),
            pltpu.VMEM((RANK // 2, 2 * RANK), F32),
            pltpu.VMEM((8, 2 * RANK), F32),
            pltpu.VMEM((8, 8, 2 * RANK), F32),
            dma((2, 2 * NY)),
            dma((6,)),
            dma((NY + 1,)),
            dma((NY + 1,)),
            dma((NY,)),
            dma((NY,)),
            dma((NZ,)),
            dma((NZ,)),
            dma((NX, NZ)),
            dma((NX, NZ)),
            dma((NY,)),
            dma((NY,)),
            dma((2 * NY,)),
            dma((2 * NY,)),
        ],
        compiler_params=pltpu.CompilerParams(
            collective_id=0, has_side_effects=True, vmem_limit_bytes=60 * 2**20
        ),
        name="sketch_scores",
    )(
        activations, hidden_grads, basis_in.T, basis_out.T, precond_out, precond_in, lengths,
        query_ids.reshape(2 * NY, -1),
    )


def solution(mesh):
    placed = (
        P("dp", "tensor"),
        P("dp", "tensor"),
        P("tensor", None),
        P("tensor", None),
        P(),
        P(),
        P("dp"),
        P(),
    )
    return jax.shard_map(
        local, mesh=mesh, in_specs=placed, out_specs=P("dp", "tensor"), check_vma=False
    )
```

```python
import jax
import jax.numpy as jnp
from jax import lax
from jax.experimental import pallas as pl
from jax.experimental.pallas import tpu as pltpu
from jax.sharding import PartitionSpec as P

MESH = pl.DeviceIdType.MESH
NX, NY, NZ = 4, 4, 8
RANK = 64
OFFSETS = (2, 1, 3, 0)
Z_ARRIVAL = (1, 7, 2, 6, 3, 5, 4)
Z_SEND = (4, 3, 5, 2, 6, 1, 7)
ORDER = ((0, 0), (0, 1), (1, 0), (2, 0), (1, 1), (2, 1), (3, 0), (3, 1))
MERGES = {3: 0, 4: 1, 5: 2, 7: 3}
WINDOW = 5
F32 = jnp.float32
BF16 = jnp.bfloat16
NN = (((1,), (0,)), ((), ()))
NT = (((1,), (1,)), ((), ()))
TN = (((0,), (0,)), ((), ()))


def split(value):
    high = value.astype(BF16)
    return high, (value - high.astype(F32)).astype(BF16)


def dot(left, right, dims):
    return lax.dot_general(left, right, dims, preferred_element_type=F32)


def dot_split(left, right, dims):
    left_high, left_low = left
    right_high, right_low = right
    return dot(left_high, right_high, dims) + (
        dot(left_high, right_low, dims) + dot(left_low, right_high, dims)
    )


def kernel(
    act_hbm, grad_hbm, basis_in_hbm, basis_out_hbm, left_hbm, right_hbm, lengths_hbm, ids_hbm,
    out_ref,
    act, grad, basis, weight, factors, lengths, ids,
    part, pair, gathered, sketch_part, sketch_pair, sketches, preconds, precond_own, score_own, scores,
    load_sem, small_sem, core_send, core_recv, swap_sem, y_send, y_recv, z_send, z_recv, x_send, x_recv,
    p_sem, f_sem,
):
    dp = lax.axis_index("dp")
    tensor = lax.axis_index("tensor")
    x, z = dp // NZ, dp % NZ
    y, core = tensor // 2, tensor % 2
    other = 1 - core

    def device(dx, dy, dz, flip):
        to_core = other if flip else core
        return (
            lax.rem(x + dx, NX) * NZ + lax.rem(z + dz, NZ),
            lax.rem(y + dy, NY) * 2 + to_core,
        )

    def remote(src, dst, send, recv, target):
        return pltpu.make_async_remote_copy(
            src_ref=src, dst_ref=dst, send_sem=send, recv_sem=recv,
            device_id=target, device_id_type=MESH,
        )

    def take(ref, sem):
        pltpu.make_async_copy(ref, ref, sem).wait()

    half = part.shape[2]
    small = [
        pltpu.make_async_copy(
            basis_in_hbm, basis.at[pl.ds(0, RANK), pl.ds(0, act.shape[1])], small_sem.at[0]
        ),
        pltpu.make_async_copy(
            basis_out_hbm,
            basis.at[pl.ds(RANK, RANK), pl.ds(act.shape[1], grad.shape[1])],
            small_sem.at[0],
        ),
        pltpu.make_async_copy(left_hbm, factors.at[pl.ds(0, RANK)], small_sem.at[1]),
        pltpu.make_async_copy(right_hbm, factors.at[pl.ds(RANK, RANK)], small_sem.at[1]),
        pltpu.make_async_copy(lengths_hbm, lengths, small_sem.at[2]),
        pltpu.make_async_copy(ids_hbm, ids, small_sem.at[3]),
    ]

    def load(index):
        step, mine = ORDER[index]
        example = lax.rem(y + OFFSETS[step], NY)
        rows = pl.ds(pl.multiple_of((example * 2 + (core if mine else other)) * half, half), half)
        slot = pl.ds(index * half, half)
        pltpu.make_async_copy(act_hbm.at[rows], act.at[slot], load_sem.at[index]).start()
        pltpu.make_async_copy(grad_hbm.at[rows], grad.at[slot], load_sem.at[index]).start()

    small[0].start()
    small[1].start()
    load(0)

    barrier = pltpu.get_barrier_semaphore()
    partners = [(0, dy, 0, flip) for dy in range(NY) for flip in (0, 1) if dy or flip]
    partners += [(0, 0, dz, 0) for dz in range(1, NZ)]
    partners += [(dx, 0, 0, 0) for dx in range(1, NX)]
    for partner in partners:
        pl.semaphore_signal(barrier, 1, device_id=device(*partner), device_id_type=MESH)

    load(1)
    basis[0:RANK, act.shape[1] :] = jnp.zeros((RANK, grad.shape[1]), BF16)
    basis[RANK:, 0 : act.shape[1]] = jnp.zeros((RANK, act.shape[1]), BF16)
    take(basis.at[pl.ds(0, RANK)], small_sem.at[0])
    for index in range(2, WINDOW):
        load(index)
    for copy in small[2:]:
        copy.start()
    weight[...] = basis[...].T

    def project(index):
        step, mine = ORDER[index]
        take(act.at[pl.ds(0, half * (act.shape[1] + grad.shape[1]) // act.shape[1])], load_sem.at[index])
        if index + WINDOW < len(ORDER):
            load(index + WINDOW)
        slot = pl.ds(index * half, half)
        part[step, mine] = dot(act[slot, :], weight[0 : act.shape[1], :], NN) + dot(
            grad[slot, :], weight[act.shape[1] :, :], NN
        )
        if not mine:
            if index == 0:
                pl.semaphore_wait(barrier, len(partners))
            to_core(step).start()

    def to_core(step):
        return remote(
            part.at[step, 0], pair.at[step], core_send, core_recv.at[step],
            device(0, 0, 0, 1),
        )

    def to_chip(step):
        return remote(
            part.at[step, 1], gathered.at[step], y_send, y_recv.at[step],
            device(0, OFFSETS[step], 0, 0),
        )

    def merge(step):
        to_core(step).wait_recv()
        part[step, 1] = part[step, 1] + pair[step]
        if OFFSETS[step]:
            to_chip(step).start()

    for index in range(len(ORDER)):
        project(index)
        if index in MERGES:
            merge(MERGES[index])

    last = len(OFFSETS) - 1
    take(factors, small_sem.at[1])
    for copy in small[4:]:
        copy.wait()
    left_split = split(factors[0:RANK, :])
    right_split = split(factors[RANK:, :])
    total = part[last, 1]
    for step in range(last):
        to_chip(step).wait_recv()
        total = total + gathered[step]
    slot = lax.broadcasted_iota(jnp.int32, total.shape, 0) + core * half
    total = jnp.where(slot < lengths[y], total, 0.0)
    total_split = split(total)
    square = dot_split(total_split, total_split, TN)
    corner = square[RANK:, 0:RANK]
    sketch_part[...] = jnp.concatenate([corner[: RANK // 2], corner[RANK // 2 :]], axis=1)
    swap = remote(
        sketch_part, sketch_pair, swap_sem.at[0], swap_sem.at[1],
        device(0, 0, 0, 1),
    )
    swap.start()
    swap.wait_recv()
    packed = sketch_part[...] + sketch_pair[...]
    sketch_pair[...] = packed

    block = RANK // 4

    def place(at_x, at_z):
        return sketches.at[pl.ds(pl.multiple_of((at_x * NZ + at_z) * block, block), block)]

    own_rows = pl.ds(pl.multiple_of(core * block, block), block)
    sketches[pl.ds(pl.multiple_of((x * NZ + z) * block, block), block), :] = sketch_pair[own_rows, :]
    own = place(x, z)

    def to_z(dz):
        return remote(own, own, z_send, z_recv.at[dz], device(0, 0, dz, 0))

    def from_z(dz):
        spot = place(x, lax.rem(z + NZ - dz, NZ))
        return remote(spot, spot, z_send, z_recv.at[dz], device(0, 0, dz, 0))

    def to_x(dx, dz):
        spot = place(x, lax.rem(z + NZ - dz, NZ))
        return remote(spot, spot, x_send, x_recv.at[dx], device(dx, 0, 0, 0))

    for dz in Z_SEND:
        to_z(dz).start()
    for dx in (2, 1, 3):
        to_x(dx, 0).start()

    whole = jnp.concatenate([packed[:, 0:RANK], packed[:, RANK:]], axis=0)
    halfway = dot_split(split(whole), right_split, NN)
    precond = dot_split(left_split, split(halfway), NN)
    precond_own[...] = jnp.concatenate([precond[: RANK // 2], precond[RANK // 2 :]], axis=1)

    def p_place(at_y):
        return preconds.at[pl.ds(pl.multiple_of(at_y * block, block), block)]

    preconds[pl.ds(pl.multiple_of(y * block, block), block), :] = precond_own[own_rows, :]

    def to_y(dy):
        return remote(p_place(y), p_place(y), p_sem.at[0], p_sem.at[1], device(0, dy, 0, 0))

    for dy in (2, 1, 3):
        to_y(dy).start()

    for dz in Z_ARRIVAL:
        from_z(dz).wait_recv()
        for dx in (2, 1, 3):
            to_x(dx, dz).start()
    take(preconds.at[pl.ds(0, (NY - 1) * block)], p_sem.at[1])
    weights = split(
        jnp.concatenate([preconds[pl.ds(row, NY, stride=block), :] for row in range(block)], axis=1)
    )
    for dx in (1, 3, 2):
        take(sketches.at[pl.ds(0, NZ * block)], x_recv.at[dx])
    rows = NX * NZ
    found = split(
        jnp.concatenate([sketches[pl.ds(row, rows, stride=block), :] for row in range(block)], axis=1)
    )
    found = [jnp.concatenate([term] * NY, axis=0) for term in found]
    lane = lax.broadcasted_iota(jnp.int32, (NY, rows * NY), 1)
    mine = jnp.where(lane // rows == y, dot_split(weights, found, NT), 0.0)

    score_own[0:NY, :] = mine
    score_own[NY:, :] = jnp.zeros((8 - NY, rows * NY), F32)

    def exchange(dy, flip):
        index = dy * 2 + flip
        return remote(
            score_own, scores.at[index], f_sem.at[0], f_sem.at[1], device(0, dy, 0, flip)
        )

    everyone = [(dy, flip) for dy in (2, 1, 3, 0) for flip in (1, 0) if dy or flip]
    for pair_to in everyone:
        exchange(*pair_to).start()
    query = ids[pl.ds(tensor, 1), :]
    spot = lax.broadcasted_iota(jnp.int32, (rows * NY, rows * NY), 0)
    onehot = jnp.where(spot % rows * NY + spot // rows == query, 1.0, 0.0).astype(BF16)
    table = score_own[...]
    take(scores.at[pl.ds(0, len(everyone))], f_sem.at[1])
    for pair_to in everyone:
        table = table + scores[pair_to[0] * 2 + pair_to[1]]
    high, low = split(table)
    lowest = (table - high.astype(F32) - low.astype(F32)).astype(BF16)
    picked = dot(high, onehot, NN) + (dot(low, onehot, NN) + dot(lowest, onehot, NN))
    out_ref[...] = picked[0:NY, :] * (1.0 / (2 * half * RANK))

    take(part.at[pl.ds(0, NY // 2)], core_send)
    take(gathered, y_send)
    take(sketch_part, swap_sem.at[0])
    take(sketches.at[pl.ds(0, (NZ - 1) * block)], z_send)
    take(sketches.at[pl.ds(0, (NX - 1) * NZ * block)], x_send)
    take(preconds.at[pl.ds(0, (NY - 1) * block)], p_sem.at[0])
    take(scores.at[pl.ds(0, len(everyone))], f_sem.at[0])


def local(
    activations, hidden_grads, basis_in, basis_out, precond_out, precond_in, lengths, query_ids
):
    tokens, features = activations.shape
    hidden = hidden_grads.shape[1]
    half = tokens // (2 * NY)
    dma = pltpu.SemaphoreType.DMA
    return pl.pallas_call(
        kernel,
        out_shape=jax.ShapeDtypeStruct((NY, query_ids.shape[0] // (2 * NY)), F32),
        in_specs=[pl.BlockSpec(memory_space=pltpu.HBM)] * 8,
        out_specs=pl.BlockSpec(memory_space=pltpu.VMEM),
        scratch_shapes=[
            pltpu.VMEM((tokens, features), BF16),
            pltpu.VMEM((tokens, hidden), BF16),
            pltpu.VMEM((2 * RANK, features + hidden), BF16),
            pltpu.VMEM((features + hidden, 2 * RANK), BF16),
            pltpu.VMEM((2 * RANK, RANK), F32),
            pltpu.SMEM((NY,), jnp.int32),
            pltpu.VMEM((2 * NY, query_ids.shape[0] // (2 * NY)), jnp.int32),
            pltpu.VMEM((NY, 2, half, 2 * RANK), F32),
            pltpu.VMEM((NY, half, 2 * RANK), F32),
            pltpu.VMEM((NY - 1, half, 2 * RANK), F32),
            pltpu.VMEM((RANK // 2, 2 * RANK), F32),
            pltpu.VMEM((RANK // 2, 2 * RANK), F32),
            pltpu.VMEM((NX * NZ * RANK // 4, 2 * RANK), F32),
            pltpu.VMEM((NY * RANK // 4, 2 * RANK), F32),
            pltpu.VMEM((RANK // 2, 2 * RANK), F32),
            pltpu.VMEM((8, 2 * RANK), F32),
            pltpu.VMEM((8, 8, 2 * RANK), F32),
            dma((len(ORDER),)),
            dma((4,)),
            dma(()),
            dma((NY,)),
            dma((2,)),
            dma(()),
            dma((NY - 1,)),
            dma(()),
            dma((NZ,)),
            dma(()),
            dma((NX,)),
            dma((2,)),
            dma((2,)),
        ],
        compiler_params=pltpu.CompilerParams(
            collective_id=0, has_side_effects=True, vmem_limit_bytes=60 * 2**20
        ),
        name="sketch_scores",
    )(
        activations, hidden_grads, basis_in.T, basis_out.T, precond_out, precond_in, lengths,
        query_ids.reshape(2 * NY, -1),
    )


def solution(mesh):
    placed = (
        P("dp", "tensor"),
        P("dp", "tensor"),
        P("tensor", None),
        P("tensor", None),
        P(),
        P(),
        P("dp"),
        P(),
    )
    return jax.shard_map(
        local, mesh=mesh, in_specs=placed, out_specs=P("dp", "tensor"), check_vma=False
    )
```

```python
import jax
import jax.numpy as jnp
from jax import lax
from jax.experimental import pallas as pl
from jax.experimental.pallas import tpu as pltpu
from jax.sharding import PartitionSpec as P

MESH = pl.DeviceIdType.MESH
NX, NY, NZ = 4, 4, 8
RANK = 64
OFFSETS = (2, 1, 3, 0)
Z_ARRIVAL = (1, 7, 2, 6, 3, 5, 4)
ORDER = ((0, 0), (0, 1), (1, 0), (2, 0), (1, 1), (2, 1), (3, 0), (3, 1))
MERGES = {2: 0, 4: 1, 5: 2}
WINDOW = 5
F32 = jnp.float32
BF16 = jnp.bfloat16
NN = (((1,), (0,)), ((), ()))
NT = (((1,), (1,)), ((), ()))
TN = (((0,), (0,)), ((), ()))


def split(value):
    high = value.astype(BF16)
    return high, (value - high.astype(F32)).astype(BF16)


def dot(left, right, dims):
    return lax.dot_general(left, right, dims, preferred_element_type=F32)


def dot_split(left, right, dims):
    left_high, left_low = left
    right_high, right_low = right
    return dot(left_high, right_high, dims) + (
        dot(left_high, right_low, dims) + dot(left_low, right_high, dims)
    )


def kernel(
    act_hbm, grad_hbm, basis_in_hbm, basis_out_hbm, left_hbm, right_hbm, lengths_hbm, ids_hbm,
    out_ref,
    act, grad, basis, weight, factors, lengths, ids,
    part, pair, relayed, gathered, sketch_part, sketch_pair, sketches, preconds, precond_own, score_own, scores,
    load_sem, small_sem, core_send, core_recv, swap_sem, relay_send, relay_recv, y_send, y_recv, z_send, z_recv, x_send, x_recv,
    p_sem, f_sem,
):
    dp = lax.axis_index("dp")
    tensor = lax.axis_index("tensor")
    x, z = dp // NZ, dp % NZ
    y, core = tensor // 2, tensor % 2
    other = 1 - core

    def others(here, size):
        return [
            lax.rem(there + (there >= here).astype(jnp.int32) - here + size, size)
            for there in range(size - 1)
        ]

    def device(dx, dy, dz, flip):
        to_core = other if flip else core
        return (
            lax.rem(x + dx, NX) * NZ + lax.rem(z + dz, NZ),
            lax.rem(y + dy, NY) * 2 + to_core,
        )

    def remote(src, dst, send, recv, target):
        return pltpu.make_async_remote_copy(
            src_ref=src, dst_ref=dst, send_sem=send, recv_sem=recv,
            device_id=target, device_id_type=MESH,
        )

    def take(ref, sem):
        pltpu.make_async_copy(ref, ref, sem).wait()

    half = part.shape[2]
    small = [
        pltpu.make_async_copy(
            basis_in_hbm, basis.at[pl.ds(0, RANK), pl.ds(0, act.shape[1])], small_sem.at[0]
        ),
        pltpu.make_async_copy(
            basis_out_hbm,
            basis.at[pl.ds(RANK, RANK), pl.ds(act.shape[1], grad.shape[1])],
            small_sem.at[0],
        ),
        pltpu.make_async_copy(left_hbm, factors.at[pl.ds(0, RANK)], small_sem.at[1]),
        pltpu.make_async_copy(right_hbm, factors.at[pl.ds(RANK, RANK)], small_sem.at[1]),
        pltpu.make_async_copy(lengths_hbm, lengths, small_sem.at[2]),
        pltpu.make_async_copy(ids_hbm, ids, small_sem.at[3]),
    ]

    def load(index):
        step, mine = ORDER[index]
        example = lax.rem(y + OFFSETS[step], NY)
        rows = pl.ds(pl.multiple_of((example * 2 + (core if mine else other)) * half, half), half)
        slot = pl.ds(index * half, half)
        pltpu.make_async_copy(act_hbm.at[rows], act.at[slot], load_sem.at[index]).start()
        pltpu.make_async_copy(grad_hbm.at[rows], grad.at[slot], load_sem.at[index]).start()

    small[0].start()
    small[1].start()
    load(0)

    barrier = pltpu.get_barrier_semaphore()
    partners = [(0, dy, 0, flip) for dy in range(NY) for flip in (0, 1) if dy or flip]
    partners += [(0, 0, dz, 0) for dz in range(1, NZ)]
    partners += [(dx, 0, 0, 0) for dx in range(1, NX)]
    for partner in partners:
        pl.semaphore_signal(barrier, 1, device_id=device(*partner), device_id_type=MESH)

    load(1)
    basis[0:RANK, act.shape[1] :] = jnp.zeros((RANK, grad.shape[1]), BF16)
    basis[RANK:, 0 : act.shape[1]] = jnp.zeros((RANK, act.shape[1]), BF16)
    take(basis.at[pl.ds(0, RANK)], small_sem.at[0])
    for index in range(2, WINDOW):
        load(index)
    for copy in small[2:]:
        copy.start()
    weight[...] = basis[...].T

    def project(index):
        step, mine = ORDER[index]
        take(act.at[pl.ds(0, half * (act.shape[1] + grad.shape[1]) // act.shape[1])], load_sem.at[index])
        if index + WINDOW < len(ORDER):
            load(index + WINDOW)
        slot = pl.ds(index * half, half)
        part[step, mine] = dot(act[slot, :], weight[0 : act.shape[1], :], NN) + dot(
            grad[slot, :], weight[act.shape[1] :, :], NN
        )
        if not mine:
            if index == 0:
                pl.semaphore_wait(barrier, len(partners))
            to_core(step).start()

    def to_core(step):
        return remote(
            part.at[step, 0], pair.at[step], core_send, core_recv.at[step],
            device(0, 0, 0, 1),
        )

    quarter = half // 2

    def to_relay(up):
        piece = pl.ds(0 if up else quarter, quarter)
        return remote(
            part.at[0, 1, piece], relayed.at[up], relay_send, relay_recv.at[up],
            device(0, 1 if up else NY - 1, 0, 0),
        )

    def to_chip(up, first):
        piece = pl.ds(0 if first else quarter, quarter)
        return remote(
            part.at[2 - up, 1, piece], gathered.at[up, piece], y_send, y_recv.at[up],
            device(0, 1 if up else NY - 1, 0, 0),
        )

    def merge(step):
        to_core(step).wait_recv()
        part[step, 1] = part[step, 1] + pair[step]
        if step == 0:
            to_relay(1).start()
            to_relay(0).start()
        elif step < 3:
            to_chip(2 - step, step == 2).start()

    def relay(up):
        piece = slice(0, quarter) if up else slice(quarter, half)
        to_relay(up).wait_recv()
        part[2 - up, 1, piece] = part[2 - up, 1, piece] + relayed[up]
        to_chip(up, up == 1).start()

    for index in range(len(ORDER)):
        project(index)
        if index in MERGES:
            merge(MERGES[index])
    relay(1)
    relay(0)
    merge(3)

    last = len(OFFSETS) - 1
    take(factors, small_sem.at[1])
    for copy in small[4:]:
        copy.wait()
    left_split = split(factors[0:RANK, :])
    right_split = split(factors[RANK:, :])
    total = part[last, 1]
    for up in (1, 0):
        take(gathered.at[up], y_recv.at[up])
        total = total + gathered[up]
    slot = lax.broadcasted_iota(jnp.int32, total.shape, 0) + core * half
    total = jnp.where(slot < lengths[y], total, 0.0)
    total_split = split(total)
    square = dot_split(total_split, total_split, TN)
    corner = square[RANK:, 0:RANK]
    sketch_part[...] = jnp.concatenate([corner[: RANK // 2], corner[RANK // 2 :]], axis=1)
    swap = remote(
        sketch_part, sketch_pair, swap_sem.at[0], swap_sem.at[1],
        device(0, 0, 0, 1),
    )
    swap.start()
    swap.wait_recv()
    packed = sketch_part[...] + sketch_pair[...]
    sketch_pair[...] = packed

    block = RANK // 4

    def place(at_x, at_z):
        return sketches.at[pl.ds(pl.multiple_of((at_x * NZ + at_z) * block, block), block)]

    own_rows = pl.ds(pl.multiple_of(core * block, block), block)
    sketches[pl.ds(pl.multiple_of((x * NZ + z) * block, block), block), :] = sketch_pair[own_rows, :]
    own = place(x, z)

    def to_z(dz):
        return remote(own, own, z_send, z_recv.at[dz], device(0, 0, dz, 0))

    def from_z(dz):
        spot = place(x, lax.rem(z + NZ - dz, NZ))
        return remote(spot, spot, z_send, z_recv.at[dz], device(0, 0, dz, 0))

    def to_x(dx, dz):
        spot = place(x, lax.rem(z + NZ - dz, NZ))
        return remote(spot, spot, x_send, x_recv.at[dx], device(dx, 0, 0, 0))

    for dz in others(z, NZ):
        to_z(dz).start()
    for dx in others(x, NX):
        to_x(dx, 0).start()

    whole = jnp.concatenate([packed[:, 0:RANK], packed[:, RANK:]], axis=0)
    halfway = dot_split(split(whole), right_split, NN)
    precond = dot_split(left_split, split(halfway), NN)
    precond_own[...] = jnp.concatenate([precond[: RANK // 2], precond[RANK // 2 :]], axis=1)

    def p_place(at_y):
        return preconds.at[pl.ds(pl.multiple_of(at_y * block, block), block)]

    preconds[pl.ds(pl.multiple_of(y * block, block), block), :] = precond_own[own_rows, :]

    def to_y(dy):
        return remote(p_place(y), p_place(y), p_sem.at[0], p_sem.at[1], device(0, dy, 0, 0))

    for dy in others(y, NY):
        to_y(dy).start()

    for dz in Z_ARRIVAL:
        from_z(dz).wait_recv()
        for dx in others(x, NX):
            to_x(dx, dz).start()
    take(preconds.at[pl.ds(0, (NY - 1) * block)], p_sem.at[1])
    weights = split(
        jnp.concatenate([preconds[pl.ds(row, NY, stride=block), :] for row in range(block)], axis=1)
    )
    for dx in (1, 3, 2):
        take(sketches.at[pl.ds(0, NZ * block)], x_recv.at[dx])
    rows = NX * NZ
    found = split(
        jnp.concatenate([sketches[pl.ds(row, rows, stride=block), :] for row in range(block)], axis=1)
    )
    mine = dot_split(weights, found, NT)
    mine = jnp.concatenate([mine, jnp.zeros((NY, rows * (NY - 1)), F32)], axis=1)
    mine = jnp.concatenate([mine, jnp.zeros((8 - NY, rows * NY), F32)], axis=0)
    mine = pltpu.roll(mine, y * rows, 1)

    score_own[...] = mine

    def exchange(change):
        target = lax.rem(tensor + change, 2 * NY)
        return remote(score_own, scores.at[change], f_sem.at[0], f_sem.at[1], (dp, target))

    for change in others(tensor, 2 * NY):
        exchange(change).start()
    query = ids[pl.ds(tensor, 1), :]
    spot = lax.broadcasted_iota(jnp.int32, (rows * NY, rows * NY), 0)
    onehot = jnp.where(spot % rows * NY + spot // rows == query, 1.0, 0.0).astype(BF16)
    table = mine
    take(scores.at[pl.ds(1, 2 * NY - 1)], f_sem.at[1])
    for change in range(1, 2 * NY):
        table = table + scores[change]
    picked = dot(jnp.concatenate(split(table), axis=0), onehot, NN)
    out_ref[...] = (picked[0:NY, :] + picked[8 : 8 + NY, :]) * (1.0 / (2 * half * RANK))

    take(part.at[pl.ds(0, NY // 2)], core_send)
    take(relayed, relay_send)
    take(gathered, y_send)
    take(sketch_part, swap_sem.at[0])
    take(sketches.at[pl.ds(0, (NZ - 1) * block)], z_send)
    take(sketches.at[pl.ds(0, (NX - 1) * NZ * block)], x_send)
    take(preconds.at[pl.ds(0, (NY - 1) * block)], p_sem.at[0])
    take(scores.at[pl.ds(1, 2 * NY - 1)], f_sem.at[0])


def local(
    activations, hidden_grads, basis_in, basis_out, precond_out, precond_in, lengths, query_ids
):
    tokens, features = activations.shape
    hidden = hidden_grads.shape[1]
    half = tokens // (2 * NY)
    dma = pltpu.SemaphoreType.DMA
    return pl.pallas_call(
        kernel,
        out_shape=jax.ShapeDtypeStruct((NY, query_ids.shape[0] // (2 * NY)), F32),
        in_specs=[pl.BlockSpec(memory_space=pltpu.HBM)] * 8,
        out_specs=pl.BlockSpec(memory_space=pltpu.VMEM),
        scratch_shapes=[
            pltpu.VMEM((tokens, features), BF16),
            pltpu.VMEM((tokens, hidden), BF16),
            pltpu.VMEM((2 * RANK, features + hidden), BF16),
            pltpu.VMEM((features + hidden, 2 * RANK), BF16),
            pltpu.VMEM((2 * RANK, RANK), F32),
            pltpu.SMEM((NY,), jnp.int32),
            pltpu.VMEM((2 * NY, query_ids.shape[0] // (2 * NY)), jnp.int32),
            pltpu.VMEM((NY, 2, half, 2 * RANK), F32),
            pltpu.VMEM((NY, half, 2 * RANK), F32),
            pltpu.VMEM((2, half // 2, 2 * RANK), F32),
            pltpu.VMEM((2, half, 2 * RANK), F32),
            pltpu.VMEM((RANK // 2, 2 * RANK), F32),
            pltpu.VMEM((RANK // 2, 2 * RANK), F32),
            pltpu.VMEM((NX * NZ * RANK // 4, 2 * RANK), F32),
            pltpu.VMEM((NY * RANK // 4, 2 * RANK), F32),
            pltpu.VMEM((RANK // 2, 2 * RANK), F32),
            pltpu.VMEM((8, 2 * RANK), F32),
            pltpu.VMEM((8, 8, 2 * RANK), F32),
            dma((len(ORDER),)),
            dma((4,)),
            dma(()),
            dma((NY,)),
            dma((2,)),
            dma(()),
            dma((2,)),
            dma(()),
            dma((2,)),
            dma(()),
            dma((NZ,)),
            dma(()),
            dma((NX,)),
            dma((2,)),
            dma((2,)),
        ],
        compiler_params=pltpu.CompilerParams(
            collective_id=0, has_side_effects=True, vmem_limit_bytes=60 * 2**20
        ),
        name="sketch_scores",
    )(
        activations, hidden_grads, basis_in.T, basis_out.T, precond_out, precond_in, lengths,
        query_ids.reshape(2 * NY, -1),
    )


def solution(mesh):
    placed = (
        P("dp", "tensor"),
        P("dp", "tensor"),
        P("tensor", None),
        P("tensor", None),
        P(),
        P(),
        P("dp"),
        P(),
    )
    return jax.shard_map(
        local, mesh=mesh, in_specs=placed, out_specs=P("dp", "tensor"), check_vma=False
    )
```

```python
import jax
import jax.numpy as jnp
from jax import lax
from jax.experimental import pallas as pl
from jax.experimental.pallas import tpu as pltpu
from jax.sharding import PartitionSpec as P

MESH = pl.DeviceIdType.MESH
NX, NY, NZ = 4, 4, 8
RANK = 64
OFFSETS = (2, 1, 3, 0)
Z_ARRIVAL = (1, 7, 2, 6, 3, 5, 4)
ORDER = ((0, 0), (0, 1), (1, 0), (2, 0), (1, 1), (2, 1), (3, 0), (3, 1))
MERGES = {2: 0, 4: 1, 5: 2}
WINDOW = 5
PIECES = 4
F32 = jnp.float32
BF16 = jnp.bfloat16
NN = (((1,), (0,)), ((), ()))
NT = (((1,), (1,)), ((), ()))
TN = (((0,), (0,)), ((), ()))


def split(value):
    high = value.astype(BF16)
    return high, (value - high.astype(F32)).astype(BF16)


def dot(left, right, dims):
    return lax.dot_general(left, right, dims, preferred_element_type=F32)


def dot_split(left, right, dims):
    left_high, left_low = left
    right_high, right_low = right
    return dot(left_high, right_high, dims) + (
        dot(left_high, right_low, dims) + dot(left_low, right_high, dims)
    )


def kernel(
    act_hbm, grad_hbm, basis_in_hbm, basis_out_hbm, left_hbm, right_hbm, lengths_hbm, ids_hbm,
    out_ref,
    act, grad, basis, weight, factors, lengths, ids,
    part, pair, relayed, gathered, sketch_part, sketch_pair, sketches, preconds, precond_own, score_own, scores,
    load_sem, small_sem, core_send, core_recv, swap_sem, relay_send, relay_recv, y_send, y_recv, z_send, z_recv, x_send, x_recv,
    p_sem, f_sem,
):
    dp = lax.axis_index("dp")
    tensor = lax.axis_index("tensor")
    x, z = dp // NZ, dp % NZ
    y, core = tensor // 2, tensor % 2
    other = 1 - core

    def others(here, size):
        return [
            lax.rem(there + (there >= here).astype(jnp.int32) - here + size, size)
            for there in range(size - 1)
        ]

    def device(dx, dy, dz, flip):
        to_core = other if flip else core
        return (
            lax.rem(x + dx, NX) * NZ + lax.rem(z + dz, NZ),
            lax.rem(y + dy, NY) * 2 + to_core,
        )

    def remote(src, dst, send, recv, target):
        return pltpu.make_async_remote_copy(
            src_ref=src, dst_ref=dst, send_sem=send, recv_sem=recv,
            device_id=target, device_id_type=MESH,
        )

    def take(ref, sem):
        pltpu.make_async_copy(ref, ref, sem).wait()

    half = part.shape[2]
    small = [
        pltpu.make_async_copy(
            basis_in_hbm, basis.at[pl.ds(0, RANK), pl.ds(0, act.shape[1])], small_sem.at[0]
        ),
        pltpu.make_async_copy(
            basis_out_hbm,
            basis.at[pl.ds(RANK, RANK), pl.ds(act.shape[1], grad.shape[1])],
            small_sem.at[0],
        ),
        pltpu.make_async_copy(left_hbm, factors.at[pl.ds(0, RANK)], small_sem.at[1]),
        pltpu.make_async_copy(right_hbm, factors.at[pl.ds(RANK, RANK)], small_sem.at[1]),
        pltpu.make_async_copy(lengths_hbm, lengths, small_sem.at[2]),
        pltpu.make_async_copy(ids_hbm, ids, small_sem.at[3]),
    ]

    def load(index):
        step, mine = ORDER[index]
        example = lax.rem(y + OFFSETS[step], NY)
        rows = pl.ds(pl.multiple_of((example * 2 + (core if mine else other)) * half, half), half)
        slot = pl.ds(index * half, half)
        pltpu.make_async_copy(act_hbm.at[rows], act.at[slot], load_sem.at[index]).start()
        pltpu.make_async_copy(grad_hbm.at[rows], grad.at[slot], load_sem.at[index]).start()

    small[0].start()
    small[1].start()
    load(0)

    barrier = pltpu.get_barrier_semaphore()
    partners = [(0, dy, 0, flip) for dy in range(NY) for flip in (0, 1) if dy or flip]
    partners += [(0, 0, dz, 0) for dz in range(1, NZ)]
    partners += [(dx, 0, 0, 0) for dx in range(1, NX)]
    for partner in partners:
        pl.semaphore_signal(barrier, 1, device_id=device(*partner), device_id_type=MESH)

    load(1)
    basis[0:RANK, act.shape[1] :] = jnp.zeros((RANK, grad.shape[1]), BF16)
    basis[RANK:, 0 : act.shape[1]] = jnp.zeros((RANK, act.shape[1]), BF16)
    take(basis.at[pl.ds(0, RANK)], small_sem.at[0])
    for index in range(2, WINDOW):
        load(index)
    for copy in small[2:]:
        copy.start()
    weight[...] = basis[...].T

    def project(index):
        step, mine = ORDER[index]
        take(act.at[pl.ds(0, half * (act.shape[1] + grad.shape[1]) // act.shape[1])], load_sem.at[index])
        if index + WINDOW < len(ORDER):
            load(index + WINDOW)
        slot = pl.ds(index * half, half)
        part[step, mine] = dot(act[slot, :], weight[0 : act.shape[1], :], NN) + dot(
            grad[slot, :], weight[act.shape[1] :, :], NN
        )
        if not mine:
            if index == 0:
                pl.semaphore_wait(barrier, len(partners))
            to_core(step).start()

    def to_core(step):
        return remote(
            part.at[step, 0], pair.at[step], core_send, core_recv.at[step],
            device(0, 0, 0, 1),
        )

    quarter = half // 2

    size = quarter // PIECES

    def to_relay(up, piece):
        rows = pl.ds((0 if up else quarter) + piece * size, size)
        return remote(
            part.at[0, 1, rows], relayed.at[up, pl.ds(piece * size, size)], relay_send,
            relay_recv.at[up, piece], device(0, 1 if up else NY - 1, 0, 0),
        )

    def to_chip(up, first):
        piece = pl.ds(0 if first else quarter, quarter)
        return remote(
            part.at[2 - up, 1, piece], gathered.at[up, piece], y_send, y_recv.at[up],
            device(0, 1 if up else NY - 1, 0, 0),
        )

    def merge(step):
        to_core(step).wait_recv()
        part[step, 1] = part[step, 1] + pair[step]
        if step == 0:
            for piece in range(PIECES):
                to_relay(1, piece).start()
                to_relay(0, piece).start()
        elif step < 3:
            to_chip(2 - step, step == 2).start()

    def relay(up, piece):
        start = (0 if up else quarter) + piece * size
        rows = slice(start, start + size)
        to_relay(up, piece).wait_recv()
        part[2 - up, 1, rows] = part[2 - up, 1, rows] + relayed[up, piece * size : (piece + 1) * size]
        cut = pl.ds(start, size)
        remote(
            part.at[2 - up, 1, cut], gathered.at[up, cut], y_send, y_recv.at[up],
            device(0, 1 if up else NY - 1, 0, 0),
        ).start()

    for index in range(len(ORDER)):
        project(index)
        if index in MERGES:
            merge(MERGES[index])
    for piece in range(PIECES):
        relay(1, piece)
        relay(0, piece)
    merge(3)

    last = len(OFFSETS) - 1
    take(factors, small_sem.at[1])
    for copy in small[4:]:
        copy.wait()
    left_split = split(factors[0:RANK, :])
    right_split = split(factors[RANK:, :])
    total = part[last, 1]
    for up in (1, 0):
        take(gathered.at[up], y_recv.at[up])
        total = total + gathered[up]
    slot = lax.broadcasted_iota(jnp.int32, total.shape, 0) + core * half
    total = jnp.where(slot < lengths[y], total, 0.0)
    total_split = split(total)
    square = dot_split(total_split, total_split, TN)
    corner = square[RANK:, 0:RANK]
    sketch_part[...] = jnp.concatenate([corner[: RANK // 2], corner[RANK // 2 :]], axis=1)
    swap = remote(
        sketch_part, sketch_pair, swap_sem.at[0], swap_sem.at[1],
        device(0, 0, 0, 1),
    )
    swap.start()
    swap.wait_recv()
    packed = sketch_part[...] + sketch_pair[...]
    sketch_pair[...] = packed

    block = RANK // 4

    def place(at_x, at_z):
        return sketches.at[pl.ds(pl.multiple_of((at_x * NZ + at_z) * block, block), block)]

    own_rows = pl.ds(pl.multiple_of(core * block, block), block)
    sketches[pl.ds(pl.multiple_of((x * NZ + z) * block, block), block), :] = sketch_pair[own_rows, :]
    own = place(x, z)

    def to_z(dz):
        return remote(own, own, z_send, z_recv.at[dz], device(0, 0, dz, 0))

    def from_z(dz):
        spot = place(x, lax.rem(z + NZ - dz, NZ))
        return remote(spot, spot, z_send, z_recv.at[dz], device(0, 0, dz, 0))

    def to_x(dx, dz):
        spot = place(x, lax.rem(z + NZ - dz, NZ))
        return remote(spot, spot, x_send, x_recv.at[dx], device(dx, 0, 0, 0))

    for dz in others(z, NZ):
        to_z(dz).start()
    for dx in others(x, NX):
        to_x(dx, 0).start()

    whole = jnp.concatenate([packed[:, 0:RANK], packed[:, RANK:]], axis=0)
    halfway = dot_split(split(whole), right_split, NN)
    precond = dot_split(left_split, split(halfway), NN)
    precond_own[...] = jnp.concatenate([precond[: RANK // 2], precond[RANK // 2 :]], axis=1)

    def p_place(at_y):
        return preconds.at[pl.ds(pl.multiple_of(at_y * block, block), block)]

    preconds[pl.ds(pl.multiple_of(y * block, block), block), :] = precond_own[own_rows, :]

    def to_y(dy):
        return remote(p_place(y), p_place(y), p_sem.at[0], p_sem.at[1], device(0, dy, 0, 0))

    for dy in others(y, NY):
        to_y(dy).start()

    for dz in Z_ARRIVAL:
        from_z(dz).wait_recv()
        for dx in others(x, NX):
            to_x(dx, dz).start()
    take(preconds.at[pl.ds(0, (NY - 1) * block)], p_sem.at[1])
    weights = split(
        jnp.concatenate([preconds[pl.ds(row, NY, stride=block), :] for row in range(block)], axis=1)
    )
    for dx in (1, 3, 2):
        take(sketches.at[pl.ds(0, NZ * block)], x_recv.at[dx])
    rows = NX * NZ
    found = split(
        jnp.concatenate([sketches[pl.ds(row, rows, stride=block), :] for row in range(block)], axis=1)
    )
    mine = dot_split(weights, found, NT)
    mine = jnp.concatenate([mine, jnp.zeros((NY, rows * (NY - 1)), F32)], axis=1)
    mine = jnp.concatenate([mine, jnp.zeros((8 - NY, rows * NY), F32)], axis=0)
    mine = pltpu.roll(mine, y * rows, 1)

    score_own[...] = mine

    def exchange(change):
        target = lax.rem(tensor + change, 2 * NY)
        return remote(score_own, scores.at[change], f_sem.at[0], f_sem.at[1], (dp, target))

    for change in others(tensor, 2 * NY):
        exchange(change).start()
    query = ids[pl.ds(tensor, 1), :]
    spot = lax.broadcasted_iota(jnp.int32, (rows * NY, rows * NY), 0)
    onehot = jnp.where(spot % rows * NY + spot // rows == query, 1.0, 0.0).astype(BF16)
    table = mine
    take(scores.at[pl.ds(1, 2 * NY - 1)], f_sem.at[1])
    for change in range(1, 2 * NY):
        table = table + scores[change]
    picked = dot(jnp.concatenate(split(table), axis=0), onehot, NN)
    out_ref[...] = (picked[0:NY, :] + picked[8 : 8 + NY, :]) * (1.0 / (2 * half * RANK))

    take(part.at[pl.ds(0, NY // 2)], core_send)
    take(relayed, relay_send)
    take(gathered, y_send)
    take(sketch_part, swap_sem.at[0])
    take(sketches.at[pl.ds(0, (NZ - 1) * block)], z_send)
    take(sketches.at[pl.ds(0, (NX - 1) * NZ * block)], x_send)
    take(preconds.at[pl.ds(0, (NY - 1) * block)], p_sem.at[0])
    take(scores.at[pl.ds(1, 2 * NY - 1)], f_sem.at[0])


def local(
    activations, hidden_grads, basis_in, basis_out, precond_out, precond_in, lengths, query_ids
):
    tokens, features = activations.shape
    hidden = hidden_grads.shape[1]
    half = tokens // (2 * NY)
    dma = pltpu.SemaphoreType.DMA
    return pl.pallas_call(
        kernel,
        out_shape=pltpu.VMEM((NY, query_ids.shape[0] // (2 * NY)), F32),
        in_specs=[pl.BlockSpec(memory_space=pltpu.HBM)] * 8,
        out_specs=pl.BlockSpec(memory_space=pltpu.VMEM),
        scratch_shapes=[
            pltpu.VMEM((tokens, features), BF16),
            pltpu.VMEM((tokens, hidden), BF16),
            pltpu.VMEM((2 * RANK, features + hidden), BF16),
            pltpu.VMEM((features + hidden, 2 * RANK), BF16),
            pltpu.VMEM((2 * RANK, RANK), F32),
            pltpu.SMEM((NY,), jnp.int32),
            pltpu.VMEM((2 * NY, query_ids.shape[0] // (2 * NY)), jnp.int32),
            pltpu.VMEM((NY, 2, half, 2 * RANK), F32),
            pltpu.VMEM((NY, half, 2 * RANK), F32),
            pltpu.VMEM((2, half // 2, 2 * RANK), F32),
            pltpu.VMEM((2, half, 2 * RANK), F32),
            pltpu.VMEM((RANK // 2, 2 * RANK), F32),
            pltpu.VMEM((RANK // 2, 2 * RANK), F32),
            pltpu.VMEM((NX * NZ * RANK // 4, 2 * RANK), F32),
            pltpu.VMEM((NY * RANK // 4, 2 * RANK), F32),
            pltpu.VMEM((RANK // 2, 2 * RANK), F32),
            pltpu.VMEM((8, 2 * RANK), F32),
            pltpu.VMEM((8, 8, 2 * RANK), F32),
            dma((len(ORDER),)),
            dma((4,)),
            dma(()),
            dma((NY,)),
            dma((2,)),
            dma(()),
            dma((2, PIECES)),
            dma(()),
            dma((2,)),
            dma(()),
            dma((NZ,)),
            dma(()),
            dma((NX,)),
            dma((2,)),
            dma((2,)),
        ],
        compiler_params=pltpu.CompilerParams(
            collective_id=0, has_side_effects=True, vmem_limit_bytes=50 * 2**20
        ),
        name="sketch_scores",
    )(
        *(
            pltpu.with_memory_space_constraint(array, pltpu.HBM)
            for array in (
                activations, hidden_grads, basis_in.T, basis_out.T, precond_out, precond_in,
                lengths, query_ids.reshape(2 * NY, -1),
            )
        )
    )


def solution(mesh):
    placed = (
        P("dp", "tensor"),
        P("dp", "tensor"),
        P("tensor", None),
        P("tensor", None),
        P(),
        P(),
        P("dp"),
        P(),
    )
    return jax.shard_map(
        local, mesh=mesh, in_specs=placed, out_specs=P("dp", "tensor"), check_vma=False
    )
```

```python
import functools

import jax
import jax.numpy as jnp
from jax import lax
from jax.experimental import pallas as pl
from jax.experimental.pallas import tpu as pltpu
from jax.sharding import PartitionSpec as P

MESH = pl.DeviceIdType.MESH
NX, NY, NZ = 4, 4, 8
RANK = 64
OFFSETS = (2, 1, 3, 0)
Z_ARRIVAL = (1, 7, 2, 6, 3, 5, 4)
ORDER = ((0, 0), (0, 1), (1, 0), (2, 0), (1, 1), (2, 1), (3, 0), (3, 1))
MERGES = {2: 0, 4: 1, 5: 2}
WINDOW = 5
DIRECT = ((0, 0),)
PIECES = 4
RELAYS = {6: (0, 1), 7: (2, 3)}
F32 = jnp.float32
BF16 = jnp.bfloat16
NN = (((1,), (0,)), ((), ()))
NT = (((1,), (1,)), ((), ()))
TN = (((0,), (0,)), ((), ()))


def split(value):
    high = value.astype(BF16)
    return high, (value - high.astype(F32)).astype(BF16)


def dot(left, right, dims):
    return lax.dot_general(left, right, dims, preferred_element_type=F32)


def dot_split(left, right, dims):
    left_high, left_low = left
    right_high, right_low = right
    return dot(left_high, right_high, dims) + (
        dot(left_high, right_low, dims) + dot(left_low, right_high, dims)
    )


def kernel(
    act_hbm, grad_hbm, basis_in_hbm, basis_out_hbm, left_hbm, right_hbm, lengths_hbm, ids_hbm,
    out_ref,
    act, grad, basis, weight, factors, lengths, ids,
    part, pair, relayed, gathered, sketch_part, sketch_pair, sketches, preconds, precond_own, score_own, scores,
    load_sem, small_sem, core_send, core_recv, swap_sem, relay_send, relay_recv, y_send, y_recv, z_send, z_recv, x_send, x_recv, direct_send,
    p_sem, f_sem,
):
    dp = lax.axis_index("dp")
    tensor = lax.axis_index("tensor")
    x, z = dp // NZ, dp % NZ
    y, core = tensor // 2, tensor % 2
    other = 1 - core

    def others(here, size):
        return [
            lax.rem(there + (there >= here).astype(jnp.int32) - here + size, size)
            for there in range(size - 1)
        ]

    def device(dx, dy, dz, flip):
        to_core = other if flip else core
        return (
            lax.rem(x + dx, NX) * NZ + lax.rem(z + dz, NZ),
            lax.rem(y + dy, NY) * 2 + to_core,
        )

    def remote(src, dst, send, recv, target):
        return pltpu.make_async_remote_copy(
            src_ref=src, dst_ref=dst, send_sem=send, recv_sem=recv,
            device_id=target, device_id_type=MESH,
        )

    def take(ref, sem):
        pltpu.make_async_copy(ref, ref, sem).wait()

    half = part.shape[2]
    small = [
        pltpu.make_async_copy(
            basis_in_hbm, basis.at[pl.ds(0, RANK), pl.ds(0, act.shape[1])], small_sem.at[0]
        ),
        pltpu.make_async_copy(
            basis_out_hbm,
            basis.at[pl.ds(RANK, RANK), pl.ds(act.shape[1], grad.shape[1])],
            small_sem.at[0],
        ),
        pltpu.make_async_copy(left_hbm, factors.at[pl.ds(0, RANK)], small_sem.at[1]),
        pltpu.make_async_copy(right_hbm, factors.at[pl.ds(RANK, RANK)], small_sem.at[1]),
        pltpu.make_async_copy(lengths_hbm, lengths, small_sem.at[2]),
        pltpu.make_async_copy(ids_hbm, ids, small_sem.at[3]),
    ]

    def load(index):
        step, mine = ORDER[index]
        example = lax.rem(y + OFFSETS[step], NY)
        rows = pl.ds(pl.multiple_of((example * 2 + (core if mine else other)) * half, half), half)
        slot = pl.ds(index * half, half)
        pltpu.make_async_copy(act_hbm.at[rows], act.at[slot], load_sem.at[index]).start()
        pltpu.make_async_copy(grad_hbm.at[rows], grad.at[slot], load_sem.at[index]).start()

    small[0].start()
    small[1].start()
    load(0)

    barrier = pltpu.get_barrier_semaphore()
    partners = [(0, dy, 0, flip) for dy in range(NY) for flip in (0, 1) if dy or flip]
    partners += [(0, 0, dz, 0) for dz in range(1, NZ)]
    partners += [(dx, 0, 0, 0) for dx in range(1, NX)]
    for partner in partners:
        pl.semaphore_signal(barrier, 1, device_id=device(*partner), device_id_type=MESH)

    def off_axes(spot):
        return jnp.logical_and(x != spot[0], z != spot[1])

    def sends_direct(target_x):
        hits = [jnp.logical_and(target_x == at_x, z == at_z) for at_x, at_z in DIRECT]
        return functools.reduce(jnp.logical_or, hits)

    @pl.when(sends_direct(x))
    def _():
        for dx in range(1, NX):
            for dz in range(1, NZ):
                pl.semaphore_signal(
                    barrier, 1, device_id=device(dx, 0, dz, 0), device_id_type=MESH
                )


    load(1)
    basis[0:RANK, act.shape[1] :] = jnp.zeros((RANK, grad.shape[1]), BF16)
    basis[RANK:, 0 : act.shape[1]] = jnp.zeros((RANK, act.shape[1]), BF16)
    take(basis.at[pl.ds(0, RANK)], small_sem.at[0])
    for index in range(2, WINDOW):
        load(index)
    for copy in small[2:]:
        copy.start()
    weight[...] = basis[...].T

    def project(index):
        step, mine = ORDER[index]
        take(act.at[pl.ds(0, half * (act.shape[1] + grad.shape[1]) // act.shape[1])], load_sem.at[index])
        if index + WINDOW < len(ORDER):
            load(index + WINDOW)
        slot = pl.ds(index * half, half)
        part[step, mine] = dot(act[slot, :], weight[0 : act.shape[1], :], NN) + dot(
            grad[slot, :], weight[act.shape[1] :, :], NN
        )
        if not mine:
            if index == 0:
                more = sum(off_axes(spot).astype(jnp.int32) for spot in DIRECT)
                pl.semaphore_wait(barrier, len(partners) + more)
            to_core(step).start()

    def to_core(step):
        return remote(
            part.at[step, 0], pair.at[step], core_send, core_recv.at[step],
            device(0, 0, 0, 1),
        )

    quarter = half // 2

    size = quarter // PIECES

    def to_relay(up, piece):
        rows = pl.ds((0 if up else quarter) + piece * size, size)
        return remote(
            part.at[0, 1, rows], relayed.at[up, pl.ds(piece * size, size)], relay_send,
            relay_recv.at[up, piece], device(0, 1 if up else NY - 1, 0, 0),
        )

    def to_chip(up, first):
        piece = pl.ds(0 if first else quarter, quarter)
        return remote(
            part.at[2 - up, 1, piece], gathered.at[up, piece], y_send, y_recv.at[up],
            device(0, 1 if up else NY - 1, 0, 0),
        )

    def merge(step):
        to_core(step).wait_recv()
        part[step, 1] = part[step, 1] + pair[step]
        if step == 0:
            for piece in range(PIECES):
                to_relay(1, piece).start()
                to_relay(0, piece).start()
        elif step < 3:
            to_chip(2 - step, step == 2).start()

    def relay(up, piece):
        start = (0 if up else quarter) + piece * size
        rows = slice(start, start + size)
        to_relay(up, piece).wait_recv()
        part[2 - up, 1, rows] = part[2 - up, 1, rows] + relayed[up, piece * size : (piece + 1) * size]
        cut = pl.ds(start, size)
        remote(
            part.at[2 - up, 1, cut], gathered.at[up, cut], y_send, y_recv.at[up],
            device(0, 1 if up else NY - 1, 0, 0),
        ).start()

    for index in range(len(ORDER)):
        project(index)
        if index in MERGES:
            merge(MERGES[index])
        for piece in RELAYS.get(index, ()):
            relay(1, piece)
            relay(0, piece)
    merge(3)

    last = len(OFFSETS) - 1
    take(factors, small_sem.at[1])
    for copy in small[4:]:
        copy.wait()
    left_split = split(factors[0:RANK, :])
    right_split = split(factors[RANK:, :])
    total = part[last, 1]
    for up in (1, 0):
        take(gathered.at[up], y_recv.at[up])
        total = total + gathered[up]
    slot = lax.broadcasted_iota(jnp.int32, total.shape, 0) + core * half
    total = jnp.where(slot < lengths[y], total, 0.0)
    total_split = split(total)
    square = dot_split(total_split, total_split, TN)
    corner = square[RANK:, 0:RANK]
    sketch_part[...] = jnp.concatenate([corner[: RANK // 2], corner[RANK // 2 :]], axis=1)
    swap = remote(
        sketch_part, sketch_pair, swap_sem.at[0], swap_sem.at[1],
        device(0, 0, 0, 1),
    )
    swap.start()
    swap.wait_recv()
    packed = sketch_part[...] + sketch_pair[...]
    sketch_pair[...] = packed

    block = RANK // 4

    def place(at_x, at_z):
        return sketches.at[pl.ds(pl.multiple_of((at_x * NZ + at_z) * block, block), block)]

    own_rows = pl.ds(pl.multiple_of(core * block, block), block)
    sketches[pl.ds(pl.multiple_of((x * NZ + z) * block, block), block), :] = sketch_pair[own_rows, :]
    own = place(x, z)

    def to_z(dz):
        return remote(own, own, z_send, z_recv.at[dz], device(0, 0, dz, 0))

    def from_z(dz):
        spot = place(x, lax.rem(z + NZ - dz, NZ))
        return remote(spot, spot, z_send, z_recv.at[dz], device(0, 0, dz, 0))

    def to_x(dx, dz):
        spot = place(x, lax.rem(z + NZ - dz, NZ))
        return remote(spot, spot, x_send, x_recv.at[dx], device(dx, 0, 0, 0))

    def to_direct(index):
        at_x, at_z = DIRECT[index]
        recv = x_recv.at[lax.rem(at_x + NX - x, NX)]
        return remote(own, own, direct_send.at[index], recv, (at_x * NZ + at_z, tensor))

    for index, spot in enumerate(DIRECT):
        pl.when(off_axes(spot))(to_direct(index).start)
    for dx in others(x, NX):
        to_x(dx, 0).start()
    for dz in others(z, NZ):
        to_z(dz).start()

    whole = jnp.concatenate([packed[:, 0:RANK], packed[:, RANK:]], axis=0)
    halfway = dot_split(split(whole), right_split, NN)
    precond = dot_split(left_split, split(halfway), NN)
    precond_own[...] = jnp.concatenate([precond[: RANK // 2], precond[RANK // 2 :]], axis=1)

    def p_place(at_y):
        return preconds.at[pl.ds(pl.multiple_of(at_y * block, block), block)]

    preconds[pl.ds(pl.multiple_of(y * block, block), block), :] = precond_own[own_rows, :]

    def to_y(dy):
        return remote(p_place(y), p_place(y), p_sem.at[0], p_sem.at[1], device(0, dy, 0, 0))

    for dy in others(y, NY):
        to_y(dy).start()

    for dz in Z_ARRIVAL:
        from_z(dz).wait_recv()
        for dx in others(x, NX):
            pl.when(jnp.logical_not(sends_direct(lax.rem(x + dx, NX))))(to_x(dx, dz).start)
    take(preconds.at[pl.ds(0, (NY - 1) * block)], p_sem.at[1])
    weights = split(
        jnp.concatenate([preconds[pl.ds(row, NY, stride=block), :] for row in range(block)], axis=1)
    )
    for dx in (1, 3, 2):
        take(sketches.at[pl.ds(0, NZ * block)], x_recv.at[dx])
    rows = NX * NZ
    found = split(
        jnp.concatenate([sketches[pl.ds(row, rows, stride=block), :] for row in range(block)], axis=1)
    )
    mine = dot_split(weights, found, NT)
    mine = jnp.concatenate([mine, jnp.zeros((NY, rows * (NY - 1)), F32)], axis=1)
    mine = jnp.concatenate([mine, jnp.zeros((8 - NY, rows * NY), F32)], axis=0)
    mine = pltpu.roll(mine, y * rows, 1)

    score_own[...] = mine

    def exchange(change):
        target = lax.rem(tensor + change, 2 * NY)
        return remote(score_own, scores.at[change], f_sem.at[0], f_sem.at[1], (dp, target))

    for change in others(tensor, 2 * NY):
        exchange(change).start()
    query = ids[pl.ds(tensor, 1), :]
    spot = lax.broadcasted_iota(jnp.int32, (rows * NY, rows * NY), 0)
    onehot = jnp.where(spot % rows * NY + spot // rows == query, 1.0, 0.0).astype(BF16)
    table = mine
    take(scores.at[pl.ds(1, 2 * NY - 1)], f_sem.at[1])
    for change in range(1, 2 * NY):
        table = table + scores[change]
    picked = dot(jnp.concatenate(split(table), axis=0), onehot, NN)
    out_ref[...] = (picked[0:NY, :] + picked[8 : 8 + NY, :]) * (1.0 / (2 * half * RANK))

    take(part.at[pl.ds(0, NY // 2)], core_send)
    take(relayed, relay_send)
    take(gathered, y_send)
    take(sketch_part, swap_sem.at[0])
    take(sketches.at[pl.ds(0, (NZ - 1) * block)], z_send)
    skips = sum(sends_direct(lax.rem(x + dx, NX)).astype(jnp.int32) for dx in range(1, NX))
    for count in range(NX):

        @pl.when(skips == count)
        def _():
            blocks = (NX - 1) * NZ - count * (NZ - 1)
            take(sketches.at[pl.ds(0, blocks * block)], x_send)

    for index, spot in enumerate(DIRECT):

        @pl.when(off_axes(spot))
        def _():
            take(sketches.at[pl.ds(0, block)], direct_send.at[index])

    take(preconds.at[pl.ds(0, (NY - 1) * block)], p_sem.at[0])
    take(scores.at[pl.ds(1, 2 * NY - 1)], f_sem.at[0])


def local(
    activations, hidden_grads, basis_in, basis_out, precond_out, precond_in, lengths, query_ids
):
    tokens, features = activations.shape
    hidden = hidden_grads.shape[1]
    half = tokens // (2 * NY)
    dma = pltpu.SemaphoreType.DMA
    return pl.pallas_call(
        kernel,
        out_shape=pltpu.VMEM((NY, query_ids.shape[0] // (2 * NY)), F32),
        in_specs=[pl.BlockSpec(memory_space=pltpu.HBM)] * 8,
        out_specs=pl.BlockSpec(memory_space=pltpu.VMEM),
        scratch_shapes=[
            pltpu.VMEM((tokens, features), BF16),
            pltpu.VMEM((tokens, hidden), BF16),
            pltpu.VMEM((2 * RANK, features + hidden), BF16),
            pltpu.VMEM((features + hidden, 2 * RANK), BF16),
            pltpu.VMEM((2 * RANK, RANK), F32),
            pltpu.SMEM((NY,), jnp.int32),
            pltpu.VMEM((2 * NY, query_ids.shape[0] // (2 * NY)), jnp.int32),
            pltpu.VMEM((NY, 2, half, 2 * RANK), F32),
            pltpu.VMEM((NY, half, 2 * RANK), F32),
            pltpu.VMEM((2, half // 2, 2 * RANK), F32),
            pltpu.VMEM((2, half, 2 * RANK), F32),
            pltpu.VMEM((RANK // 2, 2 * RANK), F32),
            pltpu.VMEM((RANK // 2, 2 * RANK), F32),
            pltpu.VMEM((NX * NZ * RANK // 4, 2 * RANK), F32),
            pltpu.VMEM((NY * RANK // 4, 2 * RANK), F32),
            pltpu.VMEM((RANK // 2, 2 * RANK), F32),
            pltpu.VMEM((8, 2 * RANK), F32),
            pltpu.VMEM((8, 8, 2 * RANK), F32),
            dma((len(ORDER),)),
            dma((4,)),
            dma(()),
            dma((NY,)),
            dma((2,)),
            dma(()),
            dma((2, PIECES)),
            dma(()),
            dma((2,)),
            dma(()),
            dma((NZ,)),
            dma(()),
            dma((NX,)),
            dma((len(DIRECT),)),
            dma((2,)),
            dma((2,)),
        ],
        compiler_params=pltpu.CompilerParams(
            collective_id=0, has_side_effects=True, vmem_limit_bytes=50 * 2**20
        ),
        name="sketch_scores",
    )(
        *(
            pltpu.with_memory_space_constraint(array, pltpu.HBM)
            for array in (
                activations, hidden_grads, basis_in.T, basis_out.T, precond_out, precond_in,
                lengths, query_ids.reshape(2 * NY, -1),
            )
        )
    )


def solution(mesh):
    placed = (
        P("dp", "tensor"),
        P("dp", "tensor"),
        P("tensor", None),
        P("tensor", None),
        P(),
        P(),
        P("dp"),
        P(),
    )
    return jax.shard_map(
        local, mesh=mesh, in_specs=placed, out_specs=P("dp", "tensor"), check_vma=False
    )
```

```python
import functools

import jax
import jax.numpy as jnp
from jax import lax
from jax.experimental import pallas as pl
from jax.experimental.pallas import tpu as pltpu
from jax.sharding import PartitionSpec as P

MESH = pl.DeviceIdType.MESH
NX, NY, NZ = 4, 4, 8
RANK = 64
OFFSETS = (2, 1, 3, 0)
Z_ARRIVAL = (1, 7, 2, 6, 3, 5, 4)
ORDER = ((0, 0), (0, 1), (1, 0), (2, 0), (1, 1), (2, 1), (3, 0), (3, 1))
MERGES = {2: 0, 4: 1, 5: 2}
WINDOW = 3
DIRECT = ((0, 0),)
PIECES = 4
RELAYS = {6: (0, 1), 7: (2, 3)}
F32 = jnp.float32
BF16 = jnp.bfloat16
NN = (((1,), (0,)), ((), ()))
NT = (((1,), (1,)), ((), ()))
TN = (((0,), (0,)), ((), ()))


def split(value):
    high = value.astype(BF16)
    return high, (value - high.astype(F32)).astype(BF16)


def dot(left, right, dims):
    return lax.dot_general(left, right, dims, preferred_element_type=F32)


def dot_split(left, right, dims):
    left_high, left_low = left
    right_high, right_low = right
    return dot(left_high, right_high, dims) + (
        dot(left_high, right_low, dims) + dot(left_low, right_high, dims)
    )


def kernel(
    act_hbm, grad_hbm, basis_in_hbm, basis_out_hbm, left_hbm, right_hbm, lengths_hbm, ids_hbm,
    out_ref,
    act, grad, basis, weight, factors, lengths, ids,
    part, pair, relayed, gathered, sketch_part, sketch_pair, sketches, preconds, precond_own, score_own, scores,
    load_sem, small_sem, core_send, core_recv, swap_sem, relay_send, relay_recv, y_send, y_recv, z_send, z_recv, x_send, x_recv, direct_send,
    p_sem, f_sem,
):
    dp = lax.axis_index("dp")
    tensor = lax.axis_index("tensor")
    x, z = dp // NZ, dp % NZ
    y, core = tensor // 2, tensor % 2
    other = 1 - core

    def others(here, size):
        return [
            lax.rem(there + (there >= here).astype(jnp.int32) - here + size, size)
            for there in range(size - 1)
        ]

    def device(dx, dy, dz, flip):
        to_core = other if flip else core
        return (
            lax.rem(x + dx, NX) * NZ + lax.rem(z + dz, NZ),
            lax.rem(y + dy, NY) * 2 + to_core,
        )

    def remote(src, dst, send, recv, target):
        return pltpu.make_async_remote_copy(
            src_ref=src, dst_ref=dst, send_sem=send, recv_sem=recv,
            device_id=target, device_id_type=MESH,
        )

    def take(ref, sem):
        pltpu.make_async_copy(ref, ref, sem).wait()

    half = part.shape[2]
    small = [
        pltpu.make_async_copy(
            basis_in_hbm, basis.at[pl.ds(0, RANK), pl.ds(0, act.shape[1])], small_sem.at[0]
        ),
        pltpu.make_async_copy(
            basis_out_hbm,
            basis.at[pl.ds(RANK, RANK), pl.ds(act.shape[1], grad.shape[1])],
            small_sem.at[0],
        ),
        pltpu.make_async_copy(left_hbm, factors.at[pl.ds(0, RANK)], small_sem.at[1]),
        pltpu.make_async_copy(right_hbm, factors.at[pl.ds(RANK, RANK)], small_sem.at[1]),
        pltpu.make_async_copy(lengths_hbm, lengths, small_sem.at[2]),
        pltpu.make_async_copy(ids_hbm, ids, small_sem.at[3]),
    ]

    def load(index):
        step, mine = ORDER[index]
        example = lax.rem(y + OFFSETS[step], NY)
        rows = pl.ds(pl.multiple_of((example * 2 + (core if mine else other)) * half, half), half)
        slot = pl.ds(index * half, half)
        pltpu.make_async_copy(act_hbm.at[rows], act.at[slot], load_sem.at[index]).start()
        pltpu.make_async_copy(grad_hbm.at[rows], grad.at[slot], load_sem.at[index]).start()

    load(0)
    small[0].start()
    small[1].start()

    barrier = pltpu.get_barrier_semaphore()
    partners = [(0, dy, 0, flip) for dy in range(NY) for flip in (0, 1) if dy or flip]
    partners += [(0, 0, dz, 0) for dz in range(1, NZ)]
    partners += [(dx, 0, 0, 0) for dx in range(1, NX)]
    for partner in partners:
        pl.semaphore_signal(barrier, 1, device_id=device(*partner), device_id_type=MESH)

    def off_axes(spot):
        return jnp.logical_and(x != spot[0], z != spot[1])

    def sends_direct(target_x):
        hits = [jnp.logical_and(target_x == at_x, z == at_z) for at_x, at_z in DIRECT]
        return functools.reduce(jnp.logical_or, hits)

    @pl.when(sends_direct(x))
    def _():
        for dx in range(1, NX):
            for dz in range(1, NZ):
                pl.semaphore_signal(
                    barrier, 1, device_id=device(dx, 0, dz, 0), device_id_type=MESH
                )


    load(1)
    basis[0:RANK, act.shape[1] :] = jnp.zeros((RANK, grad.shape[1]), BF16)
    basis[RANK:, 0 : act.shape[1]] = jnp.zeros((RANK, act.shape[1]), BF16)
    take(basis.at[pl.ds(0, RANK)], small_sem.at[0])
    for index in range(2, WINDOW):
        load(index)
    for copy in small[2:]:
        copy.start()
    weight[...] = basis[...].T

    def project(index):
        step, mine = ORDER[index]
        take(act.at[pl.ds(0, half * (act.shape[1] + grad.shape[1]) // act.shape[1])], load_sem.at[index])
        if index + WINDOW < len(ORDER):
            load(index + WINDOW)
        slot = pl.ds(index * half, half)
        part[step, mine] = dot(act[slot, :], weight[0 : act.shape[1], :], NN) + dot(
            grad[slot, :], weight[act.shape[1] :, :], NN
        )
        if not mine:
            if index == 0:
                more = sum(off_axes(spot).astype(jnp.int32) for spot in DIRECT)
                pl.semaphore_wait(barrier, len(partners) + more)
            to_core(step).start()

    def to_core(step):
        return remote(
            part.at[step, 0], pair.at[step], core_send, core_recv.at[step],
            device(0, 0, 0, 1),
        )

    quarter = half // 2

    size = quarter // PIECES

    def to_relay(up, piece):
        rows = pl.ds((0 if up else quarter) + piece * size, size)
        return remote(
            part.at[0, 1, rows], relayed.at[up, pl.ds(piece * size, size)], relay_send,
            relay_recv.at[up, piece], device(0, 1 if up else NY - 1, 0, 0),
        )

    def to_chip(up, first):
        piece = pl.ds(0 if first else quarter, quarter)
        return remote(
            part.at[2 - up, 1, piece], gathered.at[up, piece], y_send, y_recv.at[up],
            device(0, 1 if up else NY - 1, 0, 0),
        )

    def merge(step):
        to_core(step).wait_recv()
        part[step, 1] = part[step, 1] + pair[step]
        if step == 0:
            for piece in range(PIECES):
                to_relay(1, piece).start()
                to_relay(0, piece).start()
        elif step < 3:
            to_chip(2 - step, step == 2).start()

    def relay(up, piece):
        start = (0 if up else quarter) + piece * size
        rows = slice(start, start + size)
        to_relay(up, piece).wait_recv()
        part[2 - up, 1, rows] = part[2 - up, 1, rows] + relayed[up, piece * size : (piece + 1) * size]
        cut = pl.ds(start, size)
        remote(
            part.at[2 - up, 1, cut], gathered.at[up, cut], y_send, y_recv.at[up],
            device(0, 1 if up else NY - 1, 0, 0),
        ).start()

    for index in range(len(ORDER)):
        project(index)
        if index in MERGES:
            merge(MERGES[index])
        for piece in RELAYS.get(index, ()):
            relay(1, piece)
            relay(0, piece)
    merge(3)

    last = len(OFFSETS) - 1
    take(factors, small_sem.at[1])
    for copy in small[4:]:
        copy.wait()
    left_split = split(factors[0:RANK, :])
    right_split = split(factors[RANK:, :])
    total = part[last, 1]
    for up in (1, 0):
        take(gathered.at[up], y_recv.at[up])
        total = total + gathered[up]
    slot = lax.broadcasted_iota(jnp.int32, total.shape, 0) + core * half
    total = jnp.where(slot < lengths[y], total, 0.0)
    total_split = split(total)
    square = dot_split(total_split, total_split, TN)
    corner = square[RANK:, 0:RANK]
    sketch_part[...] = jnp.concatenate([corner[: RANK // 2], corner[RANK // 2 :]], axis=1)
    swap = remote(
        sketch_part, sketch_pair, swap_sem.at[0], swap_sem.at[1],
        device(0, 0, 0, 1),
    )
    swap.start()
    swap.wait_recv()
    packed = sketch_part[...] + sketch_pair[...]
    sketch_pair[...] = packed

    block = RANK // 4

    def place(at_x, at_z):
        return sketches.at[pl.ds(pl.multiple_of((at_x * NZ + at_z) * block, block), block)]

    own_rows = pl.ds(pl.multiple_of(core * block, block), block)
    sketches[pl.ds(pl.multiple_of((x * NZ + z) * block, block), block), :] = sketch_pair[own_rows, :]
    own = place(x, z)

    def to_z(dz):
        return remote(own, own, z_send, z_recv.at[dz], device(0, 0, dz, 0))

    def from_z(dz):
        spot = place(x, lax.rem(z + NZ - dz, NZ))
        return remote(spot, spot, z_send, z_recv.at[dz], device(0, 0, dz, 0))

    def to_x(dx, dz):
        spot = place(x, lax.rem(z + NZ - dz, NZ))
        return remote(spot, spot, x_send, x_recv.at[dx], device(dx, 0, 0, 0))

    def to_direct(index):
        at_x, at_z = DIRECT[index]
        recv = x_recv.at[lax.rem(at_x + NX - x, NX)]
        return remote(own, own, direct_send.at[index], recv, (at_x * NZ + at_z, tensor))

    for index, spot in enumerate(DIRECT):
        pl.when(off_axes(spot))(to_direct(index).start)
    for dx in others(x, NX):
        to_x(dx, 0).start()
    for dz in others(z, NZ):
        to_z(dz).start()

    whole = jnp.concatenate([packed[:, 0:RANK], packed[:, RANK:]], axis=0)
    halfway = dot_split(split(whole), right_split, NN)
    precond = dot_split(left_split, split(halfway), NN)
    precond_own[...] = jnp.concatenate([precond[: RANK // 2], precond[RANK // 2 :]], axis=1)

    def p_place(at_y):
        return preconds.at[pl.ds(pl.multiple_of(at_y * block, block), block)]

    preconds[pl.ds(pl.multiple_of(y * block, block), block), :] = precond_own[own_rows, :]

    def to_y(dy):
        return remote(p_place(y), p_place(y), p_sem.at[0], p_sem.at[1], device(0, dy, 0, 0))

    for dy in others(y, NY):
        to_y(dy).start()

    for dz in Z_ARRIVAL:
        from_z(dz).wait_recv()
        for dx in others(x, NX):
            pl.when(jnp.logical_not(sends_direct(lax.rem(x + dx, NX))))(to_x(dx, dz).start)
    take(preconds.at[pl.ds(0, (NY - 1) * block)], p_sem.at[1])
    weights = split(
        jnp.concatenate([preconds[pl.ds(row, NY, stride=block), :] for row in range(block)], axis=1)
    )
    for dx in (1, 3, 2):
        take(sketches.at[pl.ds(0, NZ * block)], x_recv.at[dx])
    rows = NX * NZ
    found = split(
        jnp.concatenate([sketches[pl.ds(row, rows, stride=block), :] for row in range(block)], axis=1)
    )
    mine = dot_split(weights, found, NT)
    mine = jnp.concatenate([mine, jnp.zeros((NY, rows * (NY - 1)), F32)], axis=1)
    mine = jnp.concatenate([mine, jnp.zeros((8 - NY, rows * NY), F32)], axis=0)
    mine = pltpu.roll(mine, y * rows, 1)

    score_own[...] = mine

    def exchange(change):
        target = lax.rem(tensor + change, 2 * NY)
        return remote(score_own, scores.at[change], f_sem.at[0], f_sem.at[1], (dp, target))

    for change in (4, 5, 3, 2, 6, 7, 1):
        exchange(change).start()
    query = ids[pl.ds(tensor, 1), :]
    spot = lax.broadcasted_iota(jnp.int32, (rows * NY, rows * NY), 0)
    onehot = jnp.where(spot % rows * NY + spot // rows == query, 1.0, 0.0).astype(BF16)
    table = mine
    take(scores.at[pl.ds(1, 2 * NY - 1)], f_sem.at[1])
    for change in range(1, 2 * NY):
        table = table + scores[change]
    picked = dot(jnp.concatenate(split(table), axis=0), onehot, NN)
    out_ref[...] = (picked[0:NY, :] + picked[8 : 8 + NY, :]) * (1.0 / (2 * half * RANK))

    take(part.at[pl.ds(0, NY // 2)], core_send)
    take(relayed, relay_send)
    take(gathered, y_send)
    take(sketch_part, swap_sem.at[0])
    take(sketches.at[pl.ds(0, (NZ - 1) * block)], z_send)
    skips = sum(sends_direct(lax.rem(x + dx, NX)).astype(jnp.int32) for dx in range(1, NX))
    for count in range(NX):

        @pl.when(skips == count)
        def _():
            blocks = (NX - 1) * NZ - count * (NZ - 1)
            take(sketches.at[pl.ds(0, blocks * block)], x_send)

    for index, spot in enumerate(DIRECT):

        @pl.when(off_axes(spot))
        def _():
            take(sketches.at[pl.ds(0, block)], direct_send.at[index])

    take(preconds.at[pl.ds(0, (NY - 1) * block)], p_sem.at[0])
    take(scores.at[pl.ds(1, 2 * NY - 1)], f_sem.at[0])


def local(
    activations, hidden_grads, basis_in, basis_out, precond_out, precond_in, lengths, query_ids
):
    tokens, features = activations.shape
    hidden = hidden_grads.shape[1]
    half = tokens // (2 * NY)
    dma = pltpu.SemaphoreType.DMA
    return pl.pallas_call(
        kernel,
        out_shape=pltpu.VMEM((NY, query_ids.shape[0] // (2 * NY)), F32),
        in_specs=[pl.BlockSpec(memory_space=pltpu.HBM)] * 8,
        out_specs=pl.BlockSpec(memory_space=pltpu.VMEM),
        scratch_shapes=[
            pltpu.VMEM((tokens, features), BF16),
            pltpu.VMEM((tokens, hidden), BF16),
            pltpu.VMEM((2 * RANK, features + hidden), BF16),
            pltpu.VMEM((features + hidden, 2 * RANK), BF16),
            pltpu.VMEM((2 * RANK, RANK), F32),
            pltpu.SMEM((NY,), jnp.int32),
            pltpu.VMEM((2 * NY, query_ids.shape[0] // (2 * NY)), jnp.int32),
            pltpu.VMEM((NY, 2, half, 2 * RANK), F32),
            pltpu.VMEM((NY, half, 2 * RANK), F32),
            pltpu.VMEM((2, half // 2, 2 * RANK), F32),
            pltpu.VMEM((2, half, 2 * RANK), F32),
            pltpu.VMEM((RANK // 2, 2 * RANK), F32),
            pltpu.VMEM((RANK // 2, 2 * RANK), F32),
            pltpu.VMEM((NX * NZ * RANK // 4, 2 * RANK), F32),
            pltpu.VMEM((NY * RANK // 4, 2 * RANK), F32),
            pltpu.VMEM((RANK // 2, 2 * RANK), F32),
            pltpu.VMEM((8, 2 * RANK), F32),
            pltpu.VMEM((8, 8, 2 * RANK), F32),
            dma((len(ORDER),)),
            dma((4,)),
            dma(()),
            dma((NY,)),
            dma((2,)),
            dma(()),
            dma((2, PIECES)),
            dma(()),
            dma((2,)),
            dma(()),
            dma((NZ,)),
            dma(()),
            dma((NX,)),
            dma((len(DIRECT),)),
            dma((2,)),
            dma((2,)),
        ],
        compiler_params=pltpu.CompilerParams(
            collective_id=0, has_side_effects=True, vmem_limit_bytes=50 * 2**20
        ),
        name="sketch_scores",
    )(
        *(
            pltpu.with_memory_space_constraint(array, pltpu.HBM)
            for array in (
                activations, hidden_grads, basis_in.T, basis_out.T, precond_out, precond_in,
                lengths, query_ids.reshape(2 * NY, -1),
            )
        )
    )


def solution(mesh):
    placed = (
        P("dp", "tensor"),
        P("dp", "tensor"),
        P("tensor", None),
        P("tensor", None),
        P(),
        P(),
        P("dp"),
        P(),
    )
    return jax.shard_map(
        local, mesh=mesh, in_specs=placed, out_specs=P("dp", "tensor"), check_vma=False
    )
```
